512 devices in a mesh: depth: 16 (over z_lo, x, core), row: 8 (over y), col: 4 (over z_hi).
Axes of the slice: x: 4, y: 8, z: 8 (z_hi: 4, z_lo: 2; z = z_hi * 2 + z_lo), core: 2. Of those that a mesh axis runs over, the one named last changes fastest.
Arguments:
- inputs: bfloat16 [2048, 24576], P(('depth', 'row'), 'col'), may hold values from -0.5 to 0.5
- grad_out: bfloat16 [2048, 6144], P(('depth', 'col'), 'row'), may hold values from -16 to 16
- weight: bfloat16 [4, 6144, 6144], P('col', 'depth', 'row'), may hold values from -0.078125 to 0.078125
Outputs:
- grad_inputs: bfloat16 [2048, 24576], P(('depth', 'row'), 'col')
- grad_weight: bfloat16 [4, 6144, 6144], P('col', 'depth', 'row')
The draws below stay inside these ranges and needn't reach their ends.
All inputs are finite; a program needn't handle non-finite values.
Results may differ from the reference program's by a relative error of at most 0.017.
Values may be sent and summed in bfloat16 or wider, within the bound.
No kernel may reach another device: no remote copies, remote signals or barrier semaphores. Data moves between devices by JAX's collectives and lax.ppermute only.
A program may use at most 64 MiB of HBM per device.

```python
import jax
import jax.numpy as jnp
from jax import lax

FF = 24576
D = 6144
SLAB = 128
TOKENS = 2048
N_DEPTH = 16
N_ROW = 8
N_COL = 4


def with_spikes(entries, rng, source, target, shards_of, factor):
    owner, partner = [(jnp.arange(entries.shape[dim]) // (entries.shape[dim] // shards_of)).reshape([-1 if axis == dim else 1 for axis in range(entries.ndim)]) for dim in (source, target)]
    chosen = jax.random.permutation(rng, shards_of)[partner]
    strong = (owner == chosen) | (owner == (partner + shards_of // 2) % shards_of)
    return jnp.where(strong, factor * entries, entries)


def steps_of(rng, extent, pieces, least, largest):
    def one(position, parts):
        heights = jax.random.uniform(jax.random.fold_in(jax.random.fold_in(rng, 6), position), (parts,), jnp.float32, least / len(pieces), largest / len(pieces))
        return jnp.repeat(jnp.exp(heights), extent[position] // parts).reshape((-1,) + (1,) * (len(extent) - position - 1))

    gain = one(*pieces[0])
    for cut in pieces[1:]:
        gain = gain * one(*cut)
    return gain


def normal_values(key, shape, width, reach, cuts=(), kind=jnp.bfloat16):
    entries = jax.random.normal(key, shape, jnp.float32) * width
    if len(cuts) > 0:
        entries = steps_of(key, shape, cuts, -0.22, 0.18) * entries
    return jnp.clip(entries, min=-reach, max=reach).astype(kind)


def heavy_noise(key, extent, deviation, reach, shards, heavy, held_as=jnp.bfloat16):
    drawn = deviation * jax.random.normal(key, extent, jnp.float32)
    if shards:
        drawn = drawn * steps_of(key, extent, shards, -0.22, 0.18)
    return jnp.clip(with_spikes(drawn, jax.random.fold_in(key, 3), *heavy), -reach, reach).astype(held_as)


def setup_inputs(seed: int = 0) -> dict:
    key_list = jax.random.split(jax.random.key(seed), 4)
    inputs = heavy_noise(key_list[0], (TOKENS, FF), (1.0 / (SLAB * N_DEPTH) ** 0.5), 0.5, ((0, 128), (1, 4)), (0, 1, 128, 5.5))
    grad_out = heavy_noise(key_list[1], (TOKENS, D), 1.0, 16.0, ((0, 64), (1, 8)), (1, 0, 64, 4.0))
    weight = normal_values(key_list[2], (N_COL, FF // N_COL, D), D ** -0.5, 0.078125, ((0, 4), (1, 16), (2, 8)))
    return dict(inputs=inputs, grad_out=grad_out, weight=weight)


def feature_step(carry, index, grad_out, matrix):
    feature_cols = D // N_ROW
    grads = lax.dynamic_slice_in_dim(grad_out, index * feature_cols, feature_cols, 1)
    weights = lax.dynamic_slice_in_dim(matrix, index * feature_cols, feature_cols, 1)
    partial_term = lax.dot_general(grads, weights, (((1,), (1,)), ((), ())), preferred_element_type=jnp.float32)
    rounded = lax.optimization_barrier(partial_term.astype(jnp.bfloat16))
    return carry + rounded.astype(jnp.float32)


def reference(inputs, grad_out, weight):
    matrix = weight.reshape(FF, D)

    def over_features(carry, index):
        return feature_step(carry, index, grad_out, matrix), None

    grad_inputs = lax.scan(over_features, jnp.zeros((TOKENS, FF), jnp.float32), jnp.arange(N_ROW, dtype=jnp.int32))[0]
    grad_weight = lax.dot_general(inputs, grad_out, (((0,), (0,)), ((), ())), preferred_element_type=jnp.float32)
    return grad_inputs.astype(jnp.bfloat16), grad_weight.astype(jnp.bfloat16).reshape(N_COL, FF // N_COL, D)
```

```python
import jax
import jax.numpy as jnp
from jax import lax
from jax.experimental import pallas as pl
from jax.experimental.pallas import tpu as pltpu
from jax.sharding import PartitionSpec as P

NX, NZ, NC, NY = 4, 2, 4, 8
T, F, H = 16, 768, 768


def depth_of(zl, x, core):
    return (zl * NX + x) * 2 + core


def near_groups():
    return [
        [
            (depth_of(zl, x, core) * NY + 2 * y4 + yp) * NC + c
            for c in range(NC)
            for zl in range(NZ)
            for yp in range(2)
        ]
        for x in range(NX)
        for core in range(2)
        for y4 in range(NY // 2)
    ]


def x_groups():
    return [[depth_of(zl, x, core) for x in range(NX)] for zl in range(NZ) for core in range(2)]


def token_groups():
    return [
        [
            depth_of(zl, x, core) * NY + 2 * y4 + parity
            for x in range(NX)
            for y4 in range(NY // 2)
            for zl in range(NZ)
        ]
        for core in range(2)
        for parity in range(2)
    ]


def call(kernel, out_shape, scalars, *operands):
    n = len(operands)
    return pl.pallas_call(
        kernel,
        out_shape=out_shape,
        in_specs=[pl.BlockSpec(memory_space=pltpu.SMEM)]
        + [pl.BlockSpec(memory_space=pltpu.VMEM)] * n,
        out_specs=jax.tree.map(lambda _: pl.BlockSpec(memory_space=pltpu.VMEM), out_shape),
        compiler_params=pltpu.CompilerParams(vmem_limit_bytes=48 * 1024 * 1024),
    )(scalars, *operands)


def spread_kernel(s_ref, x_ref, o_ref):
    for zl in range(NZ):
        for x in range(NX):
            block = x_ref[:, pl.ds((zl * NX + x) * H, H)]
            for y4 in range(NY // 2):
                o_ref[x, y4, zl] = block


def terms_kernel(s_ref, g_ref, own_ref, other_ref, o_ref):
    parity = s_ref[0]
    g_own = g_ref[:, parity].reshape(32 * T, F)
    g_other = g_ref[:, 1 - parity].reshape(32 * T, F)
    for half in range(2):
        total = lax.dot_general(
            g_own, own_ref[half], (((1,), (1,)), ((), ())), preferred_element_type=jnp.float32
        ) + lax.dot_general(
            g_other, other_ref[half], (((1,), (1,)), ((), ())), preferred_element_type=jnp.float32
        )
        o_ref[:, :, pl.ds(half * 384, 384)] = total.astype(jnp.bfloat16).reshape(32, T, 384)


def weight_kernel(flip, s_ref, a_ref, g_ref, o_ref):
    parity, core = s_ref[0], s_ref[1]
    h0 = pl.multiple_of((1 - core if flip else core) * 384, 384)
    acts = a_ref[:, pl.ds(h0, 384)]
    for k in range(2):
        g = g_ref[:, 1 - parity if k else parity].reshape(32 * T, F)
        o_ref[k] = lax.dot_general(
            acts, g, (((0,), (0,)), ((), ())), preferred_element_type=jnp.float32
        ).astype(o_ref.dtype)


def sum_kernel(s_ref, x_ref, o_ref):
    for zl in range(NZ):
        for x in range(NX):
            total = x_ref[x, 0, zl].astype(jnp.float32)
            for y4 in range(1, NY // 2):
                total = total + x_ref[x, y4, zl].astype(jnp.float32)
            o_ref[:, pl.ds((zl * NX + x) * H, H)] = total.astype(jnp.bfloat16)


def swap_core(x):
    return lax.ppermute(x, "depth", [(i, i ^ 1) for i in range(16)])


def swap_pair(x):
    return lax.ppermute(x, "row", [(i, i ^ 1) for i in range(8)])


def local(inputs, grad_out, weight):
    bf = jnp.bfloat16
    core = lax.axis_index("depth") % 2
    parity = lax.axis_index("row") % 2
    s = jnp.stack([parity, core]).astype(jnp.int32)

    w = weight.reshape(384, F)
    w_pair = swap_pair(w)
    near = lax.all_to_all(
        jnp.broadcast_to(grad_out.reshape(1, 2, T, F), (8, 2, T, F)).reshape(16, T, F),
        ("depth", "row", "col"),
        split_axis=0,
        concat_axis=0,
        axis_index_groups=near_groups(),
        tiled=True,
    )
    spread = call(
        spread_kernel, jax.ShapeDtypeStruct((NX, NY // 2, NZ, T, H), bf), s, inputs
    ).reshape(32, T, H)
    acts = lax.all_to_all(
        spread,
        ("depth", "row"),
        split_axis=0,
        concat_axis=0,
        axis_index_groups=token_groups(),
        tiled=True,
    ).reshape(32 * T, H)
    grads = lax.all_to_all(
        jnp.broadcast_to(near.reshape(1, 16 * T, F), (NX, 16 * T, F)),
        "depth",
        split_axis=0,
        concat_axis=0,
        axis_index_groups=x_groups(),
        tiled=True,
    ).reshape(32, 2, T, F)
    w_core, w_both = swap_core(w), swap_core(w_pair)

    def by_core(mine, theirs):
        return jnp.where(core == 0, jnp.stack([mine, theirs]), jnp.stack([theirs, mine]))

    own, other = by_core(w, w_core), by_core(w_pair, w_both)
    terms = call(terms_kernel, jax.ShapeDtypeStruct((32, T, H), bf), s, grads, own, other)
    summed = lax.all_to_all(
        terms,
        ("depth", "row"),
        split_axis=0,
        concat_axis=0,
        axis_index_groups=token_groups(),
        tiled=True,
    )

    def weight_term(flip, dtype):
        return call(
            lambda *refs: weight_kernel(flip, *refs),
            jax.ShapeDtypeStruct((2, 384, F), dtype),
            s,
            acts,
            grads,
        )

    sent = swap_core(weight_term(True, bf))
    kept = weight_term(False, jnp.float32)
    both = kept + sent.astype(jnp.float32)
    crossed = swap_pair(both[1].astype(bf))
    grad_weight = (both[0] + crossed.astype(jnp.float32)).astype(bf)
    grad_inputs = call(
        sum_kernel,
        jax.ShapeDtypeStruct((T, 8 * H), bf),
        s,
        summed.reshape(NX, NY // 2, NZ, T, H),
    )
    return grad_inputs, grad_weight.reshape(weight.shape)


def solution(mesh):
    in_specs = (P(("depth", "row"), "col"), P(("depth", "col"), "row"), P("col", "depth", "row"))
    out_specs = (P(("depth", "row"), "col"), P("col", "depth", "row"))
    return jax.shard_map(local, mesh=mesh, in_specs=in_specs, out_specs=out_specs, check_vma=False)
```

```python
import jax
import jax.numpy as jnp
from jax import lax
from jax.experimental import pallas as pl
from jax.experimental.pallas import tpu as pltpu
from jax.sharding import PartitionSpec as P

NX, NZ, NC, NY = 4, 2, 4, 8
T, F, B = 16, 768, 384


def depth_of(zl, x, core):
    return (zl * NX + x) * 2 + core


def x_groups():
    return [[depth_of(zl, x, core) for x in range(NX)] for zl in range(NZ) for core in range(2)]


def token_groups():
    return [
        [
            depth_of(zl, x, core) * NY + 2 * y4 + parity
            for x in range(NX)
            for core in range(2)
            for y4 in range(NY // 2)
        ]
        for zl in range(NZ)
        for parity in range(2)
    ]


def exchange(x, axes, groups=None):
    return lax.all_to_all(
        x, axes, split_axis=0, concat_axis=0, axis_index_groups=groups, tiled=True
    )


def call(kernel, out_shape, scalars, *operands):
    n = len(operands)
    return pl.pallas_call(
        kernel,
        out_shape=out_shape,
        in_specs=[pl.BlockSpec(memory_space=pltpu.SMEM)]
        + [pl.BlockSpec(memory_space=pltpu.VMEM)] * n,
        out_specs=jax.tree.map(lambda _: pl.BlockSpec(memory_space=pltpu.VMEM), out_shape),
        compiler_params=pltpu.CompilerParams(vmem_limit_bytes=48 * 1024 * 1024),
    )(scalars, *operands)


def spread_kernel(s_ref, x_ref, o_ref):
    for x in range(NX):
        for core in range(2):
            for zl in range(NZ):
                block = x_ref[:, pl.ds(depth_of(zl, x, core) * B, B)]
                for y4 in range(NY // 2):
                    o_ref[x, core, y4, :, pl.ds(zl * B, B)] = block


def block_at(zl):
    return pl.ds(pl.multiple_of(zl * B, B), B)


def rows_at(g_ref, parity):
    return g_ref[:, :, parity].reshape(NX * NY // 2 * T, F)


def terms_kernel(other, s_ref, g_ref, h_ref, w_ref, v_ref, o_ref):
    zl, core, parity = s_ref[0], s_ref[1], s_ref[2]
    at = 1 - parity if other else parity
    g = jnp.concatenate([rows_at(g_ref, at), rows_at(h_ref, at)], axis=0)
    for w, z in ((w_ref, zl), (v_ref, 1 - zl)):
        total = lax.dot_general(
            g, w[...], (((1,), (1,)), ((), ())), preferred_element_type=jnp.float32
        ).astype(jnp.bfloat16)
        total = total.reshape(2, NX, NY // 2, T, B)
        o_ref[:, core, :, :, block_at(z)] = total[0]
        o_ref[:, 1 - core, :, :, block_at(z)] = total[1]


def weight_product(s_ref, mine_ref, theirs_ref, g_ref, h_ref, flip_z):
    zl, core, parity = s_ref[0], s_ref[1], s_ref[2]
    at = block_at(1 - zl if flip_z else zl)
    acts = jnp.concatenate(
        [
            a[:, c, :, :, at].reshape(NX * NY // 2 * T, B)
            for c in (core, 1 - core)
            for a in (mine_ref, theirs_ref)
        ],
        axis=0,
    )
    grads = jnp.concatenate(
        [rows_at(g, p) for g in (g_ref, h_ref) for p in (parity, 1 - parity)], axis=0
    )
    return lax.dot_general(
        acts, grads, (((0,), (0,)), ((), ())), preferred_element_type=jnp.float32
    )


def weight_kernel(flip, s_ref, mine_ref, theirs_ref, g_ref, h_ref, o_ref):
    o_ref[...] = weight_product(s_ref, mine_ref, theirs_ref, g_ref, h_ref, flip).astype(o_ref.dtype)


def add_kernel(s_ref, a_ref, b_ref, o_ref):
    for i in range(NX * NY):
        o_ref[i] = a_ref[i] + b_ref[i]


def last_kernel(s_ref, a_ref, b_ref, o_ref):
    o_ref[...] = (a_ref[...] + b_ref[...].astype(jnp.float32)).astype(o_ref.dtype)


def sum_kernel(s_ref, x_ref, o_ref):
    for x in range(NX):
        for core in range(2):
            total = x_ref[x, core, 0].astype(jnp.float32)
            for y4 in range(1, NY // 2):
                total = total + x_ref[x, core, y4].astype(jnp.float32)
            for zl in range(NZ):
                o_ref[:, pl.ds(depth_of(zl, x, core) * B, B)] = total[:, zl * B : zl * B + B].astype(
                    jnp.bfloat16
                )


def swap_core(x):
    return lax.ppermute(x, "depth", [(i, i ^ 1) for i in range(16)])


def swap_z(x):
    return lax.ppermute(x, "depth", [(i, i ^ 8) for i in range(16)])


def swap_row(x):
    pairs = []
    for d in range(16):
        for y in range(NY):
            step = 1 if y % 2 == d % 2 else NY - 1
            pairs.append((d * NY + y, d * NY + (y + step) % NY))
    return lax.ppermute(x, ("depth", "row"), pairs)


def local(inputs, grad_out, weight):
    bf, f32 = jnp.bfloat16, jnp.float32
    shape = jax.ShapeDtypeStruct
    depth, row = lax.axis_index("depth"), lax.axis_index("row")
    s = jnp.stack([depth // 8, depth % 2, row % 2]).astype(jnp.int32)
    w = weight.reshape(B, F)
    half = shape((NX, 2, NY // 2, T, 2 * B), bf)
    flat = (NX * NY, T, 2 * B)

    spread = call(spread_kernel, half, s, inputs)
    mine = exchange(spread.reshape(flat), ("depth", "row"), token_groups())
    slab = lax.all_gather(grad_out, "col", axis=0, tiled=True)
    slab, w = lax.optimization_barrier((slab, w))
    w_z = swap_z(w)
    grads = lax.all_gather(slab, "depth", axis=0, tiled=True, axis_index_groups=x_groups())
    mine, grads, w_z = lax.optimization_barrier((mine, grads, w_z))
    others = swap_core(grads)
    theirs = swap_row(mine)
    grads = grads.reshape(NX, NY // 2, 2, T, F)
    others = others.reshape(NX, NY // 2, 2, T, F)

    def terms(other):
        return call(
            lambda *refs: terms_kernel(other, *refs), half, s, grads, others, w, w_z
        ).reshape(flat)

    sent = terms(True)
    got = swap_row(sent)
    theirs, sent = lax.optimization_barrier((theirs, sent))

    def weight_term(flip, dtype):
        return call(
            lambda *refs: weight_kernel(flip, *refs),
            shape((B, F), dtype),
            s,
            mine.reshape(half.shape),
            theirs.reshape(half.shape),
            grads,
            others,
        )

    far, keep = weight_term(True, bf), terms(False)
    got, far, keep = lax.optimization_barrier((got, far, keep))
    part = call(add_kernel, shape(flat, bf), s, keep, got)
    summed = exchange(part, ("depth", "row"), token_groups())
    grad_inputs = call(sum_kernel, shape((T, 16 * B), bf), s, summed.reshape(half.shape))
    grad_weight = call(last_kernel, shape((B, F), bf), s, weight_term(False, f32), swap_z(far))
    return grad_inputs, grad_weight.reshape(weight.shape)


def solution(mesh):
    in_specs = (P(("depth", "row"), "col"), P(("depth", "col"), "row"), P("col", "depth", "row"))
    out_specs = (P(("depth", "row"), "col"), P("col", "depth", "row"))
    return jax.shard_map(local, mesh=mesh, in_specs=in_specs, out_specs=out_specs, check_vma=False)
```

```python
import jax
import jax.numpy as jnp
from jax import lax
from jax.experimental import pallas as pl
from jax.experimental.pallas import tpu as pltpu
from jax.sharding import PartitionSpec as P

NX, NZ, NC, NY = 4, 2, 4, 8
T, F, B = 16, 768, 384


def depth_of(zl, x, core):
    return (zl * NX + x) * 2 + core


def x_groups():
    return [[depth_of(zl, x, core) for x in range(NX)] for zl in range(NZ) for core in range(2)]


def token_groups():
    return [
        [
            depth_of(zl, x, core) * NY + 2 * y4 + parity
            for x in range(NX)
            for core in range(2)
            for y4 in range(NY // 2)
        ]
        for zl in range(NZ)
        for parity in range(2)
    ]


def exchange(x, axes, groups=None):
    return lax.all_to_all(
        x, axes, split_axis=0, concat_axis=0, axis_index_groups=groups, tiled=True
    )


def call(kernel, out_shape, scalars, *operands, cost=None):
    n = len(operands)
    return pl.pallas_call(
        kernel,
        out_shape=out_shape,
        in_specs=[pl.BlockSpec(memory_space=pltpu.SMEM)]
        + [pl.BlockSpec(memory_space=pltpu.VMEM)] * n,
        out_specs=jax.tree.map(lambda _: pl.BlockSpec(memory_space=pltpu.VMEM), out_shape),
        compiler_params=pltpu.CompilerParams(vmem_limit_bytes=48 * 1024 * 1024),
        cost_estimate=cost and pl.CostEstimate(flops=cost, bytes_accessed=0, transcendentals=0),
    )(scalars, *operands)


def spread_kernel(s_ref, x_ref, o_ref):
    for x in range(NX):
        for core in range(2):
            for zl in range(NZ):
                block = x_ref[:, pl.ds(depth_of(zl, x, core) * B, B)]
                for y4 in range(NY // 2):
                    o_ref[x, core, y4, :, pl.ds(zl * B, B)] = block


def block_at(zl):
    return pl.ds(pl.multiple_of(zl * B, B), B)


def rows_at(g_ref, parity):
    return g_ref[:, :, parity].reshape(NX * NY // 2 * T, F)


def terms_kernel(other, s_ref, g_ref, h_ref, w_ref, v_ref, o_ref):
    zl, core, parity = s_ref[0], s_ref[1], s_ref[2]
    at = 1 - parity if other else parity
    g = jnp.concatenate([rows_at(g_ref, at), rows_at(h_ref, at)], axis=0)
    for w, z in ((w_ref, zl), (v_ref, 1 - zl)):
        total = lax.dot_general(
            g, w[...], (((1,), (1,)), ((), ())), preferred_element_type=jnp.float32
        ).astype(jnp.bfloat16)
        total = total.reshape(2, NX, NY // 2, T, B)
        o_ref[:, core, :, :, block_at(z)] = total[0]
        o_ref[:, 1 - core, :, :, block_at(z)] = total[1]


def weight_product(s_ref, mine_ref, theirs_ref, g_ref, h_ref, flip_z):
    zl, core, parity = s_ref[0], s_ref[1], s_ref[2]
    at = block_at(1 - zl if flip_z else zl)
    acts = jnp.concatenate(
        [
            a[:, c, :, :, at].reshape(NX * NY // 2 * T, B)
            for c in (core, 1 - core)
            for a in (mine_ref, theirs_ref)
        ],
        axis=0,
    )
    grads = jnp.concatenate(
        [rows_at(g, p) for g in (g_ref, h_ref) for p in (parity, 1 - parity)], axis=0
    )
    return lax.dot_general(
        acts, grads, (((0,), (0,)), ((), ())), preferred_element_type=jnp.float32
    )


def weight_kernel(flip, s_ref, mine_ref, theirs_ref, g_ref, h_ref, o_ref):
    o_ref[...] = weight_product(s_ref, mine_ref, theirs_ref, g_ref, h_ref, flip).astype(o_ref.dtype)


def add_kernel(s_ref, a_ref, b_ref, o_ref):
    for i in range(NX * NY):
        o_ref[i] = a_ref[i] + b_ref[i]


def last_kernel(s_ref, a_ref, b_ref, o_ref):
    o_ref[...] = (a_ref[...] + b_ref[...].astype(jnp.float32)).astype(o_ref.dtype)


def sum_kernel(s_ref, x_ref, o_ref):
    for x in range(NX):
        for core in range(2):
            total = x_ref[x, core, 0].astype(jnp.float32)
            for y4 in range(1, NY // 2):
                total = total + x_ref[x, core, y4].astype(jnp.float32)
            for zl in range(NZ):
                o_ref[:, pl.ds(depth_of(zl, x, core) * B, B)] = total[:, zl * B : zl * B + B].astype(
                    jnp.bfloat16
                )


def swap_core(x):
    return lax.ppermute(x, "depth", [(i, i ^ 1) for i in range(16)])


def swap_z(x):
    return lax.ppermute(x, "depth", [(i, i ^ 8) for i in range(16)])


def swap_row(x):
    pairs = []
    for d in range(16):
        for y in range(NY):
            step = 1 if y % 2 == d % 2 else NY - 1
            pairs.append((d * NY + y, d * NY + (y + step) % NY))
    return lax.ppermute(x, ("depth", "row"), pairs)


def local(inputs, grad_out, weight):
    bf, f32 = jnp.bfloat16, jnp.float32
    shape = jax.ShapeDtypeStruct
    depth, row = lax.axis_index("depth"), lax.axis_index("row")
    s = jnp.stack([depth // 8, depth % 2, row % 2]).astype(jnp.int32)
    w = weight.reshape(B, F)
    half = shape((NX, 2, NY // 2, T, 2 * B), bf)
    flat = (NX * NY, T, 2 * B)

    spread = call(spread_kernel, half, s, inputs)
    mine = exchange(spread.reshape(flat), ("depth", "row"), token_groups())
    slab = lax.all_gather(grad_out, "col", axis=0, tiled=True)
    slab, w = lax.optimization_barrier((slab, w))
    w_z = swap_z(w)
    grads = lax.all_gather(slab, "depth", axis=0, tiled=True, axis_index_groups=x_groups())
    mine, grads, w_z = lax.optimization_barrier((mine, grads, w_z))
    others = swap_core(grads)
    grads = grads.reshape(NX, NY // 2, 2, T, F)
    others = others.reshape(NX, NY // 2, 2, T, F)

    def terms(other):
        return call(
            lambda *refs: terms_kernel(other, *refs), half, s, grads, others, w, w_z
        ).reshape(flat)

    sent = terms(True)
    got = swap_row(sent)
    mine, sent = lax.optimization_barrier((mine, sent))
    theirs = swap_row(mine)

    def weight_term(flip, dtype, cost=None):
        return call(
            lambda *refs: weight_kernel(flip, *refs),
            shape((B, F), dtype),
            s,
            mine.reshape(half.shape),
            theirs.reshape(half.shape),
            grads,
            others,
            cost=cost,
        )

    part = call(add_kernel, shape(flat, bf), s, terms(False), got)
    summed = exchange(part, ("depth", "row"), token_groups())
    grad_inputs = call(sum_kernel, shape((T, 16 * B), bf), s, summed.reshape(half.shape))
    crossed = swap_z(weight_term(True, bf, 10**10))
    grad_weight = call(last_kernel, shape((B, F), bf), s, weight_term(False, f32), crossed)
    return grad_inputs, grad_weight.reshape(weight.shape)


def solution(mesh):
    in_specs = (P(("depth", "row"), "col"), P(("depth", "col"), "row"), P("col", "depth", "row"))
    out_specs = (P(("depth", "row"), "col"), P("col", "depth", "row"))
    return jax.shard_map(local, mesh=mesh, in_specs=in_specs, out_specs=out_specs, check_vma=False)
```

```python
import jax
import jax.numpy as jnp
from jax import lax
from jax.experimental import pallas as pl
from jax.experimental.pallas import tpu as pltpu
from jax.sharding import PartitionSpec as P

NX, NZ, NC, NY = 4, 2, 4, 8
T, F, B = 16, 768, 384


def depth_of(zl, x, core):
    return (zl * NX + x) * 2 + core


def x_groups():
    return [[depth_of(zl, x, core) for x in range(NX)] for zl in range(NZ) for core in range(2)]


def token_groups():
    return [
        [
            depth_of(zl, x, core) * NY + 2 * y4 + parity
            for x in range(NX)
            for core in range(2)
            for y4 in range(NY // 2)
        ]
        for zl in range(NZ)
        for parity in range(2)
    ]


def exchange(x, axes, groups=None):
    return lax.all_to_all(
        x, axes, split_axis=0, concat_axis=0, axis_index_groups=groups, tiled=True
    )


def call(kernel, out_shape, scalars, *operands, cost=None):
    n = len(operands)
    return pl.pallas_call(
        kernel,
        out_shape=out_shape,
        in_specs=[pl.BlockSpec(memory_space=pltpu.SMEM)]
        + [pl.BlockSpec(memory_space=pltpu.VMEM)] * n,
        out_specs=jax.tree.map(lambda _: pl.BlockSpec(memory_space=pltpu.VMEM), out_shape),
        compiler_params=pltpu.CompilerParams(vmem_limit_bytes=48 * 1024 * 1024),
        cost_estimate=cost and pl.CostEstimate(flops=cost, bytes_accessed=0, transcendentals=0),
    )(scalars, *operands)


def spread_rows(x):
    blocks = [
        jnp.concatenate(
            [x[:, depth_of(zl, i, core) * B : (depth_of(zl, i, core) + 1) * B] for zl in range(NZ)],
            axis=1,
        )
        for i in range(NX)
        for core in range(2)
    ]
    one = jnp.stack(blocks).reshape(NX, 2, 1, T, 2 * B)
    return jnp.broadcast_to(one, (NX, 2, NY // 2, T, 2 * B))


def block_at(zl):
    return pl.ds(pl.multiple_of(zl * B, B), B)


def rows_at(g_ref, parity):
    return g_ref[:, :, parity].reshape(NX * NY // 2 * T, F)


def terms_kernel(other, s_ref, g_ref, h_ref, w_ref, v_ref, o_ref):
    zl, core, parity = s_ref[0], s_ref[1], s_ref[2]
    at = 1 - parity if other else parity
    g = jnp.concatenate([rows_at(g_ref, at), rows_at(h_ref, at)], axis=0)
    for w, z in ((w_ref, zl), (v_ref, 1 - zl)):
        total = lax.dot_general(
            g, w[...], (((1,), (1,)), ((), ())), preferred_element_type=jnp.float32
        ).astype(jnp.bfloat16)
        total = total.reshape(2, NX, NY // 2, T, B)
        o_ref[:, core, :, :, block_at(z)] = total[0]
        o_ref[:, 1 - core, :, :, block_at(z)] = total[1]


def weight_product(s_ref, mine_ref, theirs_ref, g_ref, h_ref, flip_z):
    zl, core, parity = s_ref[0], s_ref[1], s_ref[2]
    at = block_at(1 - zl if flip_z else zl)
    acts = jnp.concatenate(
        [
            a[:, c, :, :, at].reshape(NX * NY // 2 * T, B)
            for c in (core, 1 - core)
            for a in (mine_ref, theirs_ref)
        ],
        axis=0,
    )
    grads = jnp.concatenate(
        [rows_at(g, p) for g in (g_ref, h_ref) for p in (parity, 1 - parity)], axis=0
    )
    return lax.dot_general(
        acts, grads, (((0,), (0,)), ((), ())), preferred_element_type=jnp.float32
    )


def weight_kernel(flip, s_ref, mine_ref, theirs_ref, g_ref, h_ref, o_ref):
    o_ref[...] = weight_product(s_ref, mine_ref, theirs_ref, g_ref, h_ref, flip).astype(o_ref.dtype)


def last_kernel(s_ref, a_ref, b_ref, o_ref):
    o_ref[...] = (a_ref[...] + b_ref[...].astype(jnp.float32)).astype(o_ref.dtype)


def sum_kernel(s_ref, x_ref, o_ref):
    for x in range(NX):
        for core in range(2):
            total = x_ref[x, core, 0].astype(jnp.float32)
            for y4 in range(1, NY // 2):
                total = total + x_ref[x, core, y4].astype(jnp.float32)
            for zl in range(NZ):
                o_ref[:, pl.ds(depth_of(zl, x, core) * B, B)] = total[:, zl * B : zl * B + B].astype(
                    jnp.bfloat16
                )


def swap_core(x):
    return lax.ppermute(x, "depth", [(i, i ^ 1) for i in range(16)])


def swap_z(x):
    return lax.ppermute(x, "depth", [(i, i ^ 8) for i in range(16)])


def swap_row(x):
    pairs = []
    for d in range(16):
        for y in range(NY):
            step = 1 if y % 2 == d % 2 else NY - 1
            pairs.append((d * NY + y, d * NY + (y + step) % NY))
    return lax.ppermute(x, ("depth", "row"), pairs)


def local(inputs, grad_out, weight):
    bf, f32 = jnp.bfloat16, jnp.float32
    shape = jax.ShapeDtypeStruct
    depth, row = lax.axis_index("depth"), lax.axis_index("row")
    s = jnp.stack([depth // 8, depth % 2, row % 2]).astype(jnp.int32)
    w = weight.reshape(B, F)
    half = shape((NX, 2, NY // 2, T, 2 * B), bf)
    flat = (NX * NY, T, 2 * B)

    spread = spread_rows(inputs)
    mine = exchange(spread.reshape(flat), ("depth", "row"), token_groups())
    slab = lax.all_gather(grad_out, "col", axis=0, tiled=True)
    slab, w = lax.optimization_barrier((slab, w))
    w_z = swap_z(w)
    grads = lax.all_gather(slab, "depth", axis=0, tiled=True, axis_index_groups=x_groups())
    mine, grads, w_z = lax.optimization_barrier((mine, grads, w_z))
    others = swap_core(grads)
    grads = grads.reshape(NX, NY // 2, 2, T, F)
    others = others.reshape(NX, NY // 2, 2, T, F)

    def terms(other):
        return call(
            lambda *refs: terms_kernel(other, *refs), half, s, grads, others, w, w_z
        ).reshape(flat)

    sent = terms(True)
    got = swap_row(sent)
    mine, sent = lax.optimization_barrier((mine, sent))
    theirs = swap_row(mine)

    def weight_term(flip, dtype, cost=None):
        return call(
            lambda *refs: weight_kernel(flip, *refs),
            shape((B, F), dtype),
            s,
            mine.reshape(half.shape),
            theirs.reshape(half.shape),
            grads,
            others,
            cost=cost,
        )

    part = terms(False) + got
    summed = exchange(part, ("depth", "row"), token_groups())
    grad_inputs = call(sum_kernel, shape((T, 16 * B), bf), s, summed.reshape(half.shape))
    crossed = swap_z(weight_term(True, bf, 10**10))
    grad_weight = call(last_kernel, shape((B, F), bf), s, weight_term(False, f32), crossed)
    return grad_inputs, grad_weight.reshape(weight.shape)


def solution(mesh):
    in_specs = (P(("depth", "row"), "col"), P(("depth", "col"), "row"), P("col", "depth", "row"))
    out_specs = (P(("depth", "row"), "col"), P("col", "depth", "row"))
    return jax.shard_map(local, mesh=mesh, in_specs=in_specs, out_specs=out_specs, check_vma=False)
```

```python
import jax
import jax.numpy as jnp
from jax import lax
from jax.experimental import pallas as pl
from jax.experimental.pallas import tpu as pltpu
from jax.sharding import PartitionSpec as P

NX, NZ, NC, NY = 4, 2, 4, 8
T, F, B = 16, 768, 384


def depth_of(zl, x, core):
    return (zl * NX + x) * 2 + core


def x_groups():
    return [[depth_of(zl, x, core) for x in range(NX)] for zl in range(NZ) for core in range(2)]


def token_groups():
    return [
        [
            depth_of(zl, x, core) * NY + 2 * y4 + parity
            for x in range(NX)
            for core in range(2)
            for y4 in range(NY // 2)
        ]
        for zl in range(NZ)
        for parity in range(2)
    ]


def exchange(x, axes, groups=None):
    return lax.all_to_all(
        x, axes, split_axis=0, concat_axis=0, axis_index_groups=groups, tiled=True
    )


def call(kernel, out_shape, scalars, *operands, cost=None):
    n = len(operands)
    return pl.pallas_call(
        kernel,
        out_shape=out_shape,
        in_specs=[pl.BlockSpec(memory_space=pltpu.SMEM)]
        + [pl.BlockSpec(memory_space=pltpu.VMEM)] * n,
        out_specs=jax.tree.map(lambda _: pl.BlockSpec(memory_space=pltpu.VMEM), out_shape),
        compiler_params=pltpu.CompilerParams(vmem_limit_bytes=48 * 1024 * 1024),
        cost_estimate=cost and pl.CostEstimate(flops=cost, bytes_accessed=0, transcendentals=0),
    )(scalars, *operands)


def spread_rows(x):
    blocks = [
        jnp.concatenate(
            [x[:, depth_of(zl, i, core) * B : (depth_of(zl, i, core) + 1) * B] for zl in range(NZ)],
            axis=1,
        )
        for i in range(NX)
        for core in range(2)
    ]
    one = jnp.stack(blocks).reshape(NX, 2, 1, T, 2 * B)
    return jnp.broadcast_to(one, (NX, 2, NY // 2, T, 2 * B))


def block_at(zl):
    return pl.ds(pl.multiple_of(zl * B, B), B)


def rows_at(g_ref, parity):
    return g_ref[:, :, parity].reshape(NX * NY // 2 * T, F)


def terms_kernel(other, s_ref, g_ref, h_ref, w_ref, v_ref, o_ref):
    zl, core, parity = s_ref[0], s_ref[1], s_ref[2]
    at = 1 - parity if other else parity
    for rows, c in ((g_ref, core), (h_ref, 1 - core)):
        g = rows_at(rows, at)
        for w, z in ((w_ref, zl), (v_ref, 1 - zl)):
            total = lax.dot_general(
                g, w[...], (((1,), (1,)), ((), ())), preferred_element_type=jnp.float32
            ).astype(jnp.bfloat16)
            o_ref[:, c, :, :, block_at(z)] = total.reshape(NX, NY // 2, T, B)


def weight_product(s_ref, mine_ref, theirs_ref, g_ref, h_ref, flip_z):
    zl, core, parity = s_ref[0], s_ref[1], s_ref[2]
    at = block_at(1 - zl if flip_z else zl)
    acts = jnp.concatenate(
        [
            a[:, c, :, :, at].reshape(NX * NY // 2 * T, B)
            for c in (core, 1 - core)
            for a in (mine_ref, theirs_ref)
        ],
        axis=0,
    )
    grads = jnp.concatenate(
        [rows_at(g, p) for g in (g_ref, h_ref) for p in (parity, 1 - parity)], axis=0
    )
    return lax.dot_general(
        acts, grads, (((0,), (0,)), ((), ())), preferred_element_type=jnp.float32
    )


def weight_kernel(flip, s_ref, mine_ref, theirs_ref, g_ref, h_ref, o_ref):
    o_ref[...] = weight_product(s_ref, mine_ref, theirs_ref, g_ref, h_ref, flip).astype(o_ref.dtype)


def last_kernel(s_ref, a_ref, b_ref, o_ref):
    o_ref[...] = (a_ref[...] + b_ref[...].astype(jnp.float32)).astype(o_ref.dtype)


def sum_kernel(s_ref, x_ref, o_ref):
    for x in range(NX):
        for core in range(2):
            total = x_ref[x, core, 0].astype(jnp.float32)
            for y4 in range(1, NY // 2):
                total = total + x_ref[x, core, y4].astype(jnp.float32)
            for zl in range(NZ):
                o_ref[:, pl.ds(depth_of(zl, x, core) * B, B)] = total[:, zl * B : zl * B + B].astype(
                    jnp.bfloat16
                )


def swap_core(x):
    return lax.ppermute(x, "depth", [(i, i ^ 1) for i in range(16)])


def swap_z(x):
    return lax.ppermute(x, "depth", [(i, i ^ 8) for i in range(16)])


def swap_row(x):
    pairs = []
    for d in range(16):
        for y in range(NY):
            step = 1 if y % 2 == d % 2 else NY - 1
            pairs.append((d * NY + y, d * NY + (y + step) % NY))
    return lax.ppermute(x, ("depth", "row"), pairs)


def local(inputs, grad_out, weight):
    bf, f32 = jnp.bfloat16, jnp.float32
    shape = jax.ShapeDtypeStruct
    depth, row = lax.axis_index("depth"), lax.axis_index("row")
    s = jnp.stack([depth // 8, depth % 2, row % 2]).astype(jnp.int32)
    w = weight.reshape(B, F)
    half = shape((NX, 2, NY // 2, T, 2 * B), bf)
    flat = (NX * NY, T, 2 * B)

    spread = spread_rows(inputs)
    mine = exchange(spread.reshape(flat), ("depth", "row"), token_groups())
    slab = lax.all_gather(grad_out, "col", axis=0, tiled=True)
    slab, w = lax.optimization_barrier((slab, w))
    w_z = swap_z(w)
    grads = lax.all_gather(slab, "depth", axis=0, tiled=True, axis_index_groups=x_groups())
    mine, grads, w_z = lax.optimization_barrier((mine, grads, w_z))
    others = swap_core(grads)
    grads = grads.reshape(NX, NY // 2, 2, T, F)
    others = others.reshape(NX, NY // 2, 2, T, F)

    def terms(other):
        return call(
            lambda *refs: terms_kernel(other, *refs), half, s, grads, others, w, w_z
        ).reshape(flat)

    sent = terms(True)
    got = swap_row(sent)
    mine, sent = lax.optimization_barrier((mine, sent))
    theirs = swap_row(mine)

    def weight_term(flip, dtype, cost=None):
        return call(
            lambda *refs: weight_kernel(flip, *refs),
            shape((B, F), dtype),
            s,
            mine.reshape(half.shape),
            theirs.reshape(half.shape),
            grads,
            others,
            cost=cost,
        )

    part = terms(False) + got
    summed = exchange(part, ("depth", "row"), token_groups())
    grad_inputs = call(sum_kernel, shape((T, 16 * B), bf), s, summed.reshape(half.shape))
    crossed = swap_z(weight_term(True, bf, 10**10))
    grad_weight = call(last_kernel, shape((B, F), bf), s, weight_term(False, f32), crossed)
    return grad_inputs, grad_weight.reshape(weight.shape)


def solution(mesh):
    in_specs = (P(("depth", "row"), "col"), P(("depth", "col"), "row"), P("col", "depth", "row"))
    out_specs = (P(("depth", "row"), "col"), P("col", "depth", "row"))
    return jax.shard_map(local, mesh=mesh, in_specs=in_specs, out_specs=out_specs, check_vma=False)
```
